32 devices in a mesh: replica: 2 (over x), side: 4 (over y, core), tp: 4 (over z).
Axes of the slice: x: 2, y: 2, z: 4, core: 2. Of those that a mesh axis runs over, the one named last changes fastest.
Arguments:
- queries: bfloat16 [4096, 4096], P(('replica', 'side'), 'tp'), parts along dimension 0, may hold values from -60 to 60
- new_keys: bfloat16 [4096, 512], P(('replica', 'side')), parts along dimension 0, may hold values from -6 to 6
- new_values: bfloat16 [4096, 512], P(('replica', 'side')), parts along dimension 0, may hold values from -6 to 6
- cache_keys: bfloat16 [8, 512, 512], P(('replica', 'side'), 'tp'), parts along dimension 0, may hold values from -6 to 6
- cache_values: bfloat16 [8, 512, 512], P(('replica', 'side'), 'tp'), parts along dimension 0, may hold values from -6 to 6
- out_weight: bfloat16 [4096, 2048], P('tp'), may hold values from -0.09375 to 0.09375
- residual: bfloat16 [4096, 2048], P(('replica', 'side', 'tp')), parts along dimension 0, may hold values from -40 to 40
- norm_gain: bfloat16 [2048], replicated, may hold values from 0.099609375 to 1.8984375
- gate_weight: bfloat16 [16, 2048, 768], P(('side', 'tp')), may hold values from -0.125 to 0.125
- up_weight: bfloat16 [16, 2048, 768], P(('side', 'tp')), may hold values from -0.125 to 0.125
- down_weight: bfloat16 [16, 768, 2048], P(('side', 'tp')), may hold values from -0.21875 to 0.21875
- expert_ids: int32 [4096, 8], P(('replica', 'side', 'tp')), parts along dimension 0, may hold values from 0 to 15, all different within a row; in each aligned block of 128 rows (0 to 127, 128 to 255, ...) at most 128 rows name the same one
- numerators: int32 [4096, 8], P(('replica', 'side', 'tp')), parts along dimension 0, may hold values from 1 to 32767
Outputs:
- output: float32 [4096, 2048], P(('replica', 'side', 'tp')), parts along dimension 0
The draws below stay inside these ranges and needn't reach their ends.
There are 2 independent parts, one for each index of `replica`. The reference program is written for one: setup_inputs(seed, part) draws one part's arguments, and reference() takes and returns one part's arrays. A program takes and returns all parts, laid end to end along the dimension named above; an argument that names none is the same for every part. Nothing has to cross between parts.
Inputs may be any that keep to these rules, and one draw needn't show every extreme that they name: `expert_ids`: each row names 8 different experts. Among the rows of one device (aligned blocks of 128 rows) no expert is named by more than 128 rows, and in every draw some expert is named by exactly 128 rows of some device.
All inputs are finite; a program needn't handle non-finite values.
Results may differ from the reference program's by a relative error of at most 0.0035.
Values may be sent and summed in bfloat16 or wider, within the bound.
A program may use at most 128 MiB of HBM per device.

```python
import math
import jax
import jax.numpy as jnp
import numpy as np
from jax import lax

D = 2048
FF = 768
H = 32
KV = 4
HD = 128
TOP = 8
CACHE_LEN = 512
TOK_GRP = 512
EXPERTS = 16
GROUPS = 4
TOKENS = 2048
ROWS_DEV = 128
CAP = 128


def shared_keys(key):
    base_key = jax.random.fold_in(key, 17)
    key_rows = jnp.clip(jax.random.normal(base_key, (GROUPS, CACHE_LEN, KV * HD), jnp.float32), -5.0, 5.0)
    return key_rows


def draw_cache_keys(key, part):
    return shared_keys(key).astype(jnp.bfloat16)


def draw_queries(key, part):
    base_key = jax.random.fold_in(key, 29)
    return jnp.clip(1.5 * jax.random.normal(base_key, (TOKENS, H * HD), jnp.float32), -9.0, 9.0).astype(jnp.bfloat16)


def draw_residual(key, part):
    base_key = jax.random.fold_in(key, 41)
    drawn = jnp.clip(jax.random.normal(base_key, (TOKENS, D), jnp.float32), -4.0, 4.0)
    return drawn.astype(jnp.bfloat16)


def set_ends(array, stream_key, low, high):
    place = [jax.random.randint(jax.random.fold_in(stream_key, axis), (), 0, length) for axis, length in enumerate(array.shape)]
    main_axis = array.shape.index(max(array.shape))
    next_to = place[:main_axis] + [(place[main_axis] + 1) % array.shape[main_axis]] + place[main_axis + 1:]
    return array.at[tuple(place)].set(low).at[tuple(next_to)].set(high)


def steps_of(rng, extent, shards, least, top_value):
    def one(axis_at, shards_of):
        heights = jax.random.uniform(jax.random.fold_in(jax.random.fold_in(rng, 6), axis_at), (shards_of,), jnp.float32, least / len(shards), top_value / len(shards))
        return jnp.repeat(jnp.exp(heights), extent[axis_at] // shards_of).reshape((-1,) + (1,) * (len(extent) - axis_at - 1))

    gain = one(*shards[0])
    for cut in shards[1:]:
        gain = gain * one(*cut)
    return gain


def deal_out(key, own, number, rows, count, top, reach, lean):
    ranking = jax.random.permutation(key, count)
    crowded, common = load_shares(count, rows * top, reach, lean, True), load_shares(count, rows * top, reach, lean, False)
    places = jnp.arange(count)

    def named(tallies, rotation):
        used = int((tallies > 0).sum())
        fixed = max(1, used // 4)
        moved = fixed + (places - fixed + rotation * (used - fixed)) % max(1, count - fixed)
        return jnp.zeros((count,), jnp.int32).at[ranking[jnp.where(places < fixed, places, moved)]].set(jnp.asarray(tallies, jnp.int32))

    tallies = jnp.where(number % 4 == 0, named(crowded, number // 4), named(common, number - number // 4 - 1))
    mixed = jax.random.permutation(jax.random.fold_in(own, 3), count)
    giver, receiver = mixed[0:count // 2 * 2:2], mixed[1:count // 2 * 2:2]
    margin = jnp.minimum(tallies[giver] - 1, reach - tallies[receiver]) // 2
    margin = jnp.where((giver == ranking[0]) | (receiver == ranking[0]) | (tallies[receiver] == 0), 0, jnp.maximum(margin, 0))
    moved = jax.random.randint(jax.random.fold_in(own, 4), (count // 2,), 0, 1 << 20) % (margin + 1)
    tallies = tallies.at[giver].add(-moved).at[receiver].add(moved)
    labels = jnp.searchsorted(jnp.cumsum(tallies), jnp.arange(rows * top), side="right").astype(jnp.int32)
    table = labels.reshape(top, rows).T
    table = table[jax.random.permutation(jax.random.fold_in(own, 1), rows)]
    rotation = jax.random.randint(jax.random.fold_in(own, 2), (rows, 1), 0, top)
    return jnp.take_along_axis(table, (jnp.arange(top)[None, :] + rotation) % top, axis=1)


def load_shares(amount, total, limit, lean, full):
    loads = [(1 << 20) // math.isqrt(rank ** lean) + 1 for rank in range(1, amount + 1)]
    largest = limit if full else min(limit, max(-(-total // amount), total * loads[0] // sum(loads)))
    least = 1 if total - largest >= amount - 1 else 0
    given, rest = [largest] + [least] * (amount - 1), total - largest - least * (amount - 1)
    while rest > 0:
        candidates = [i for i in range(1, amount) if given[i] < largest] or [i for i in range(1, amount) if given[i] < limit]
        mass, remaining = sum([loads[i] for i in candidates]), rest
        for i in candidates:
            addition = min(limit - given[i], max(1, remaining * loads[i] // mass), rest)
            given[i] = given[i] + addition
            rest = rest - addition
    return np.array(given)


def noise(stream_key, dims, spread, most, pieces=(), kind=jnp.bfloat16):
    array = spread * jax.random.normal(stream_key, dims, jnp.float32)
    if pieces:
        array = array * steps_of(stream_key, dims, pieces, -0.22, 0.18)
    return jnp.clip(array, -most, most).astype(kind)


def setup_inputs(seed: int = 0, part: int = 0) -> dict:
    key_of = jax.random.split(jax.random.key(seed), 14)
    part_splits = jax.random.split(jax.random.fold_in(key_of[13], part), 14)
    queries = draw_queries(jax.random.fold_in(jax.random.fold_in(key_of[13], part), 71), part)
    new_keys = noise(part_splits[1], (TOKENS, KV * HD), 1.0, 6.0, ((0, 4),))
    new_values = noise(part_splits[2], (TOKENS, KV * HD), 1.0, 6.0, ((0, 4),))
    cache_keys = draw_cache_keys(jax.random.fold_in(jax.random.fold_in(key_of[13], part), 71), part)
    cache_values = noise(part_splits[4], (GROUPS, CACHE_LEN, KV * HD), 1.0, 6.0, ((0, 4), (1, 4)))
    out_weight = noise(key_of[5], (H * HD, D), (H * HD) ** -0.5, 0.09375, ((0, 4),))
    residual = draw_residual(jax.random.fold_in(jax.random.fold_in(key_of[13], part), 71), part)
    norm_gain = jnp.clip(1.0 + 0.18 * jax.random.normal(key_of[7], (D,), jnp.float32), 0.099609375, 1.8984375).astype(jnp.bfloat16)
    gate_weight = noise(key_of[8], (EXPERTS, D, FF), D ** -0.5, 0.125, ((0, 16),))
    up_weight = noise(key_of[9], (EXPERTS, D, FF), D ** -0.5, 0.125, ((0, 16),))
    down_weight = noise(key_of[10], (EXPERTS, FF, D), FF ** -0.5, 0.21875, ((0, 16),))
    expert_ids_keys = jax.random.split(jax.random.fold_in(part_splits[11], 1), TOKENS // ROWS_DEV)
    expert_ids_turns = jax.random.permutation(jax.random.fold_in(part_splits[11], 3), TOKENS // ROWS_DEV)
    expert_ids = jax.vmap(lambda own, number: deal_out(jax.random.fold_in(part_splits[11], 2), own, number, ROWS_DEV, EXPERTS, TOP, CAP, 2))(expert_ids_keys, expert_ids_turns).reshape((TOKENS, TOP))
    numerators = set_ends(jax.random.randint(part_splits[12], (TOKENS, TOP), 1, 32768), jax.random.fold_in(part_splits[12], 1), 1, 32767).astype(jnp.int32)
    return dict(queries=queries, new_keys=new_keys, new_values=new_values, cache_keys=cache_keys, cache_values=cache_values, out_weight=out_weight, residual=residual, norm_gain=norm_gain, gate_weight=gate_weight, up_weight=up_weight, down_weight=down_weight, expert_ids=expert_ids, numerators=numerators)


def attend_group(operands):
    group_queries, group_keys, group_values, stored_keys, stored_values = operands
    kv_repeat = H // KV
    key_rows = jnp.concatenate([stored_keys, group_keys], axis=0).reshape(CACHE_LEN + TOK_GRP, KV, HD)
    value_rows = jnp.concatenate([stored_values, group_values], axis=0).reshape(CACHE_LEN + TOK_GRP, KV, HD)
    key_rows = jnp.repeat(key_rows, kv_repeat, axis=1).astype(jnp.float32)
    value_rows = jnp.repeat(value_rows, kv_repeat, axis=1).astype(jnp.float32)
    query_heads = group_queries.reshape(TOK_GRP, H, HD).astype(jnp.float32)
    scores = jnp.einsum('rhd,nhd->hrn', query_heads, key_rows, precision=lax.Precision.HIGHEST) / math.sqrt(HD)
    position = jnp.arange(TOK_GRP)[:, None]
    column = jnp.arange(CACHE_LEN + TOK_GRP)[None, :]
    visible = column <= position + CACHE_LEN
    scores = jnp.where(visible[None], scores, -1e+30)
    highest = lax.optimization_barrier(jnp.max(scores, axis=-1, keepdims=True))
    exponent = jnp.exp(scores - highest)
    totals = lax.optimization_barrier(jnp.sum(exponent, axis=-1))
    probs = lax.optimization_barrier(exponent.astype(jnp.bfloat16)).astype(jnp.float32)
    context = jnp.einsum('hrn,nhd->hrd', probs, value_rows, precision=lax.Precision.HIGHEST) / totals[..., None]
    return context.transpose(1, 0, 2).reshape(TOK_GRP, H * HD).astype(jnp.bfloat16)

def reference(queries, new_keys, new_values, cache_keys, cache_values, out_weight, residual, norm_gain, gate_weight, up_weight, down_weight, expert_ids, numerators):
    grouped = lax.map(attend_group, (queries.reshape(GROUPS, TOK_GRP, H * HD), new_keys.reshape(GROUPS, TOK_GRP, KV * HD), new_values.reshape(GROUPS, TOK_GRP, KV * HD), cache_keys, cache_values))
    context_all = grouped.reshape(TOKENS, H * HD)
    stream = residual.astype(jnp.float32) + jnp.dot(context_all, out_weight, preferred_element_type=jnp.float32)
    normed = (stream * lax.rsqrt(lax.optimization_barrier(jnp.mean(stream * stream, axis=-1, keepdims=True)) + 1e-06) * norm_gain.astype(jnp.float32)).astype(jnp.bfloat16)
    tile_rows = 128
    copies = TOKENS * TOP
    flat_ids = expert_ids.reshape(copies).astype(jnp.int32)
    owners = (jnp.arange(copies) // TOP).astype(jnp.int32)
    sort_order = jnp.argsort(flat_ids, stable=True).astype(jnp.int32)
    sorted_ids = flat_ids[sort_order]
    counts = jnp.zeros((EXPERTS,), jnp.int32).at[flat_ids].add(1)
    starts = (jnp.cumsum(counts) - counts).astype(jnp.int32)
    slot_rank = (jnp.arange(copies).astype(jnp.int32) - starts[sorted_ids]).astype(jnp.int32)
    padded = ((counts + tile_rows - 1) // tile_rows * tile_rows).astype(jnp.int32)
    tile_start = (jnp.cumsum(padded) - padded).astype(jnp.int32)
    placed_at = (tile_start[sorted_ids] + slot_rank).astype(jnp.int32)
    tile_count = (copies + tile_rows - 1) // tile_rows + EXPERTS
    source = jnp.zeros((tile_count * tile_rows,), jnp.int32).at[placed_at].set(owners[sort_order])
    tile_first = (jnp.arange(tile_count) * tile_rows).astype(jnp.int32)
    tile_expert = (lax.optimization_barrier(jnp.sum((tile_start[None, :] <= tile_first[:, None]).astype(jnp.int32), axis=1)) - 1).astype(jnp.int32)

    def run_tile(tile_args):
        sources, expert = tile_args
        selected = normed[sources]
        gate_sum = jnp.dot(selected, gate_weight[expert], preferred_element_type=jnp.float32)
        up_sum = jnp.dot(selected, up_weight[expert], preferred_element_type=jnp.float32)
        hidden = (jax.nn.silu(gate_sum) * up_sum).astype(jnp.bfloat16)
        return jnp.dot(hidden, down_weight[expert], preferred_element_type=jnp.float32).astype(jnp.bfloat16)
    tile_outputs = lax.map(run_tile, (source.reshape(tile_count, tile_rows), tile_expert))
    results = tile_outputs.reshape(tile_count * tile_rows, D)[placed_at]
    per_copy = jnp.zeros((copies, D), jnp.bfloat16).at[sort_order].set(results)
    weights = numerators.astype(jnp.float32)
    weights = weights / lax.optimization_barrier(jnp.sum(weights, axis=1, keepdims=True))
    mixture = lax.optimization_barrier(jnp.sum(weights[:, :, None] * per_copy.reshape(TOKENS, TOP, D).astype(jnp.float32), axis=1))
    return stream + mixture
```

```python
import math

import jax
import jax.numpy as jnp
from jax import lax
from jax.sharding import PartitionSpec as P

D = 2048
H = 32
KV = 4
HD = 128


def pick_heads(block_rows, head_kv):
    length_now = block_rows.shape[0]
    shaped = block_rows.reshape(length_now, KV, HD)
    return jnp.take(shaped, head_kv, axis=1)


def softmax_update(state_now, scores, values):
    running, totals, context = state_now
    highest = jnp.maximum(running, jnp.max(scores, axis=-1))
    factor = jnp.exp(running - highest)
    exponent = jnp.exp(scores - highest[..., None])
    totals = totals * factor + jnp.sum(exponent, axis=-1)
    context = context * factor[..., None] + jnp.einsum(
        "hrn,nhd->hrd", exponent.astype(jnp.bfloat16), values, preferred_element_type=jnp.float32
    )
    return (highest, totals, context)


def dense_experts(
    stream, normed, gate_weight, up_weight, down_weight, expert_ids, numerators, experts_all
):
    weights = numerators.astype(jnp.float32)
    weights = weights / jnp.sum(weights, axis=1, keepdims=True)
    named = expert_ids[:, :, None] == jnp.arange(experts_all)[None, None, :]
    per_expert = jnp.sum(jnp.where(named, weights[:, :, None], 0.0), axis=1)
    all_weights = lax.all_gather(per_expert, ("side", "tp"), axis=0, tiled=True)
    me = lax.axis_index(("side", "tp"))
    own_weight = lax.dynamic_slice_in_dim(all_weights, me, 1, axis=1)
    rows = lax.all_gather(normed, ("side", "tp"), axis=0, tiled=True)
    gate_sum = jnp.dot(rows, gate_weight[0], preferred_element_type=jnp.float32)
    upward = jnp.dot(rows, up_weight[0], preferred_element_type=jnp.float32)
    hidden = (jax.nn.silu(gate_sum) * upward).astype(jnp.bfloat16)
    expert_out = jnp.dot(hidden, down_weight[0], preferred_element_type=jnp.float32)
    weighted = (expert_out * own_weight).astype(jnp.bfloat16)
    mixture = lax.psum_scatter(weighted, ("side", "tp"), scatter_dimension=0, tiled=True)
    return stream + mixture.astype(jnp.float32)


def local(
    queries,
    new_keys,
    new_values,
    cache_keys,
    cache_values,
    out_weight,
    residual,
    norm_gain,
    gate_weight,
    up_weight,
    down_weight,
    expert_ids,
    numerators,
):
    tp_count = lax.axis_size("tp")
    side_count = lax.axis_size("side")
    group_rows = queries.shape[0]
    local_heads = queries.shape[1] // HD
    head_kv = (lax.axis_index("tp") * local_heads + jnp.arange(local_heads)) // (H // KV)
    query_heads = queries.reshape(group_rows, local_heads, HD)
    score_scale = 1.0 / math.sqrt(HD)
    initial = (
        jnp.full((local_heads, group_rows), -1e30, jnp.float32),
        jnp.zeros((local_heads, group_rows), jnp.float32),
        jnp.zeros((local_heads, group_rows, HD), jnp.float32),
    )
    cache_both = lax.all_gather(
        jnp.concatenate([cache_keys[0], cache_values[0]], axis=1), "tp", axis=0, tiled=True
    )
    key_width = cache_keys.shape[2]
    key_piece = pick_heads(cache_both[:, :key_width], head_kv)
    value_piece = pick_heads(cache_both[:, key_width:], head_kv)
    scores = (
        jnp.einsum("rhd,nhd->hrn", query_heads, key_piece, preferred_element_type=jnp.float32)
        * score_scale
    )
    state_now = softmax_update(initial, scores, value_piece)
    own_keys = pick_heads(new_keys, head_kv)
    own_values = pick_heads(new_values, head_kv)
    scores = (
        jnp.einsum("rhd,nhd->hrn", query_heads, own_keys, preferred_element_type=jnp.float32)
        * score_scale
    )
    positions = jnp.arange(group_rows)
    visible = positions[None, :] <= positions[:, None]
    scores = jnp.where(visible[None], scores, -1e30)
    running, totals, context = softmax_update(state_now, scores, own_values)
    attended = (
        (context / totals[..., None])
        .transpose(1, 0, 2)
        .reshape(group_rows, local_heads * HD)
        .astype(jnp.bfloat16)
    )
    own_rows = residual.shape[0]
    attn_out = lax.psum_scatter(
        jnp.dot(attended, out_weight, preferred_element_type=jnp.float32).astype(jnp.bfloat16),
        "tp",
        scatter_dimension=0,
        tiled=True,
    ).astype(jnp.float32)
    stream = residual.astype(jnp.float32) + attn_out
    normed = (
        stream
        * lax.rsqrt(jnp.mean(stream * stream, axis=-1, keepdims=True) + 1e-06)
        * norm_gain.astype(jnp.float32)
    ).astype(jnp.bfloat16)
    experts_all = side_count * tp_count
    top_count = expert_ids.shape[1]
    copies = own_rows * top_count
    capacity = max(2, 2 * copies // experts_all)
    if capacity >= own_rows:
        return dense_experts(
            stream, normed, gate_weight, up_weight, down_weight, expert_ids, numerators, experts_all
        )
    flat_ids = expert_ids.reshape(copies)
    one_hot = (flat_ids[:, None] == jnp.arange(experts_all)[None, :]).astype(jnp.int32)
    earlier = jnp.cumsum(one_hot, axis=0) - one_hot
    slot_rank = jnp.sum(earlier * one_hot, axis=1)
    slot_index = flat_ids * capacity + slot_rank
    owners = jnp.arange(copies) // top_count
    outgoing = (
        jnp.zeros((experts_all * capacity, D), jnp.bfloat16).at[slot_index].set(normed[owners])
    )
    outgoing = outgoing.reshape(experts_all, capacity, D)
    buffer = lax.all_to_all(outgoing, ("side", "tp"), split_axis=0, concat_axis=0, tiled=True)
    buffer_shape = buffer.shape
    flat_rows = buffer.reshape(-1, D)
    gate_sum = jnp.dot(flat_rows, gate_weight[0], preferred_element_type=jnp.float32)
    upward = jnp.dot(flat_rows, up_weight[0], preferred_element_type=jnp.float32)
    hidden = (jax.nn.silu(gate_sum) * upward).astype(jnp.bfloat16)
    returned = lax.all_to_all(
        jnp.dot(hidden, down_weight[0], preferred_element_type=jnp.float32)
        .astype(jnp.bfloat16)
        .reshape(buffer_shape),
        ("side", "tp"),
        split_axis=0,
        concat_axis=0,
        tiled=True,
    )
    gathered = returned.reshape(experts_all * capacity, D)[slot_index]
    weights = numerators.astype(jnp.float32)
    weights = weights / jnp.sum(weights, axis=1, keepdims=True)
    mixture = jnp.sum(
        weights[:, :, None] * gathered.reshape(own_rows, top_count, D).astype(jnp.float32), axis=1
    )
    return stream + mixture


def solution(mesh):
    in_specs = (
        P(("replica", "side"), "tp"),
        P(("replica", "side"), None),
        P(("replica", "side"), None),
        P(("replica", "side"), "tp", None),
        P(("replica", "side"), "tp", None),
        P("tp", None),
        P(("replica", "side", "tp"), None),
        P(),
        P(("side", "tp"), None, None),
        P(("side", "tp"), None, None),
        P(("side", "tp"), None, None),
        P(("replica", "side", "tp"), None),
        P(("replica", "side", "tp"), None),
    )
    out_specs = P(("replica", "side", "tp"), None)
    return jax.shard_map(local, mesh=mesh, in_specs=in_specs, out_specs=out_specs, check_vma=False)
```

```python
import functools
import math

import jax
import jax.numpy as jnp
from jax import lax
from jax.experimental import pallas as pl
from jax.experimental.pallas import tpu as pltpu
from jax.sharding import PartitionSpec as P

D = 2048
H = 32
KV = 4
HD = 128
MESH = pl.DeviceIdType.MESH


def pick_heads(block_rows, head_kv):
    length_now = block_rows.shape[0]
    shaped = block_rows.reshape(length_now, KV, HD)
    return jnp.take(shaped, head_kv, axis=1)


def softmax_update(state_now, scores, values):
    running, totals, context = state_now
    highest = jnp.maximum(running, jnp.max(scores, axis=-1))
    factor = jnp.exp(running - highest)
    exponent = jnp.exp(scores - highest[..., None])
    totals = totals * factor + jnp.sum(exponent, axis=-1)
    context = context * factor[..., None] + jnp.einsum(
        "hrn,nhd->hrd", exponent.astype(jnp.bfloat16), values, preferred_element_type=jnp.float32
    )
    return (highest, totals, context)


def piece(length, most):
    return most if length % most == 0 else length


def near_first(at, step, count):
    found = jnp.int32(0)
    for place in range(count):
        order = sorted(range(count), key=lambda other: (abs(other - place), other))
        for turn in range(count):
            hit = jnp.logical_and(at == place, step == turn)
            found = found + jnp.where(hit, order[turn], 0)
    return found


def experts_kernel(
    side_count, tp_count, own_ref, weight_ref, gate_hbm, up_hbm, down_hbm, mix_ref,
    rows, parts, from_core, from_y, from_z, gate, up, down, hidden,
    load_sem, row_recv, up_send, down_send, y_send, core_send,
    core1_send, core1_recv, y1_send, y1_recv, z1_send, z1_recv,
):
    side, z = lax.axis_index("side"), lax.axis_index("tp")
    y, core = side // 2, side % 2
    other_y, other_core = side + 2 - 4 * y, side + 1 - 2 * core
    far_core = other_y + 1 - 2 * core
    own_rows, width = own_ref.shape
    inner = gate.shape[1]
    loads = [
        pltpu.make_async_copy(source.at[0], target, load_sem.at[at])
        for at, (source, target) in enumerate(((gate_hbm, gate), (up_hbm, up), (down_hbm, down)))
    ]
    for load in loads:
        load.start()

    barrier = pltpu.get_barrier_semaphore()
    for step in range(1, tp_count):
        pl.semaphore_signal(
            barrier, inc=1, device_id={"tp": lax.rem(z + step, tp_count)}, device_id_type=MESH
        )
    for target in (other_y, other_core):
        pl.semaphore_signal(barrier, inc=1, device_id={"side": target}, device_id_type=MESH)
    pl.semaphore_wait(barrier, tp_count + 1)

    def send_row(at_side, at_z, send_sem, target):
        return pltpu.make_async_remote_copy(
            src_ref=rows.at[at_side, at_z],
            dst_ref=rows.at[at_side, at_z],
            send_sem=send_sem,
            recv_sem=row_recv.at[at_side, at_z],
            device_id=target,
            device_id_type=MESH,
        )

    def wait_row(at_side, at_z):
        send_row(at_side, at_z, up_send.at[at_z], {"side": other_core}).wait_recv()

    def line_sends(at_z):
        return (
            (
                jnp.logical_and(at_z <= z, z < tp_count - 1),
                send_row(side, at_z, up_send.at[at_z], {"tp": jnp.minimum(z + 1, tp_count - 1)}),
            ),
            (
                jnp.logical_and(at_z >= z, z > 0),
                send_row(side, at_z, down_send.at[at_z], {"tp": jnp.maximum(z - 1, 0)}),
            ),
        )

    def side_sends(at_z):
        return (
            send_row(side, at_z, y_send.at[at_z], {"side": other_y}),
            send_row(side, at_z, core_send.at[0, at_z], {"side": other_core}),
        )

    def pass_on(at_z):
        return send_row(other_y, at_z, core_send.at[1, at_z], {"side": other_core})

    def spread(at_z):
        for condition, copy in line_sends(at_z):
            pl.when(condition)(copy.start)
        for copy in side_sends(at_z):
            copy.start()

    def to_core(at_y, at_z):
        return pltpu.make_async_remote_copy(
            src_ref=parts.at[2 * at_y + 1 - core, at_z],
            dst_ref=from_core.at[at_y, at_z],
            send_sem=core1_send.at[at_y, at_z],
            recv_sem=core1_recv.at[at_y, at_z],
            device_id={"side": other_core},
            device_id_type=MESH,
        )

    def to_y(at_z):
        return pltpu.make_async_remote_copy(
            src_ref=parts.at[other_y, at_z],
            dst_ref=from_y.at[at_z],
            send_sem=y1_send.at[at_z],
            recv_sem=y1_recv.at[at_z],
            device_id={"side": other_y},
            device_id_type=MESH,
        )

    def to_line(at_z, slot, target):
        return pltpu.make_async_remote_copy(
            src_ref=parts.at[side, at_z],
            dst_ref=from_z.at[slot],
            send_sem=z1_send.at[at_z],
            recv_sem=z1_recv.at[slot],
            device_id={"tp": target},
            device_id_type=MESH,
        )

    def add_to_part(at_side, at_z, arrived):
        parts[at_side, at_z] = (
            parts[at_side, at_z].astype(jnp.float32) + arrived[...].astype(jnp.float32)
        ).astype(jnp.bfloat16)

    rows[side, z] = own_ref[...]
    spread(z)
    for load in loads:
        load.wait()

    def forward(step, carry):
        at_z = near_first(z, step, tp_count)

        @pl.when(step + 1 < tp_count)
        def _():
            next_z = near_first(z, step + 1, tp_count)
            wait_row(side, next_z)
            spread(next_z)

        wait_row(other_y, at_z)
        pass_on(at_z).start()
        wait_row(other_core, at_z)
        wait_row(far_core, at_z)
        count = side_count * own_rows
        block = piece(inner, 256)

        def hide(at, carry):
            columns = pl.ds(pl.multiple_of(at * block, block), block)
            taken = rows[:, at_z].reshape(count, width)
            gate_sum = jnp.dot(taken, gate[:, columns], preferred_element_type=jnp.float32)
            upward = jnp.dot(taken, up[:, columns], preferred_element_type=jnp.float32)
            hidden[:, columns] = (gate_sum / (1.0 + jnp.exp(-gate_sum)) * upward).astype(
                jnp.bfloat16
            )
            return carry

        lax.fori_loop(0, inner // block, hide, 0)
        out_block = piece(width, 512)

        def show(at, carry):
            columns = pl.ds(pl.multiple_of(at * out_block, out_block), out_block)
            out = jnp.dot(hidden[...], down[:, columns], preferred_element_type=jnp.float32)
            scale = weight_ref[:, at_z].reshape(count, 1)
            parts[:, at_z, :, columns] = (
                (out * scale).astype(jnp.bfloat16).reshape(side_count, own_rows, out_block)
            )
            return carry

        lax.fori_loop(0, width // out_block, show, 0)
        for at_y in range(side_count // 2):
            to_core(at_y, at_z).start()
        return carry

    lax.fori_loop(0, tp_count, forward, 0)

    def back_y(step, carry):
        at_z = near_first(z, tp_count - 1 - step, tp_count)
        to_core(1 - y, at_z).wait_recv()
        add_to_part(other_y, at_z, from_core.at[1 - y, at_z])
        to_y(at_z).start()
        to_core(y, at_z).wait_recv()
        add_to_part(side, at_z, from_core.at[y, at_z])
        return carry

    lax.fori_loop(0, tp_count, back_y, 0)

    def back_z(step, carry):
        at_z = near_first(z, tp_count - 1 - step, tp_count)
        to_y(at_z).wait_recv()
        add_to_part(side, at_z, from_y.at[at_z])
        to_line(at_z, z, at_z).start()
        return carry

    lax.fori_loop(0, tp_count - 1, back_z, 0)
    to_y(z).wait_recv()
    mix_ref[...] = parts[side, z].astype(jnp.float32) + from_y[z].astype(jnp.float32)

    def collect(step, carry):
        at_z = near_first(z, step, tp_count)
        to_line(at_z, at_z, at_z).wait_recv()
        mix_ref[...] += from_z[at_z].astype(jnp.float32)
        return carry

    lax.fori_loop(1, tp_count, collect, 0)

    def drain(at_z, carry):
        for condition, copy in line_sends(at_z):
            pl.when(condition)(copy.wait_send)
        for copy in side_sends(at_z):
            copy.wait_send()
        pass_on(at_z).wait_send()
        for at_y in range(side_count // 2):
            to_core(at_y, at_z).wait_send()
        to_y(at_z).wait_send()
        pl.when(at_z != z)(to_line(at_z, z, at_z).wait_send)
        return carry

    lax.fori_loop(0, tp_count, drain, 0)


def exchange_experts(normed, own_weight, gate_weight, up_weight, down_weight):
    side_count, tp_count = lax.axis_size("side"), lax.axis_size("tp")
    own_rows, width = normed.shape
    inner = gate_weight.shape[2]
    half = side_count // 2
    dma = pltpu.SemaphoreType.DMA
    block = (own_rows, width)
    flops = 6 * side_count * tp_count * own_rows * width * inner
    return pl.pallas_call(
        functools.partial(experts_kernel, side_count, tp_count),
        out_shape=jax.ShapeDtypeStruct(block, jnp.float32),
        in_specs=[pl.BlockSpec(memory_space=pltpu.VMEM)] * 2
        + [pl.BlockSpec(memory_space=pl.ANY)] * 3,
        out_specs=pl.BlockSpec(memory_space=pltpu.VMEM),
        scratch_shapes=[
            pltpu.VMEM((side_count, tp_count) + block, jnp.bfloat16),
            pltpu.VMEM((side_count, tp_count) + block, jnp.bfloat16),
            pltpu.VMEM((half, tp_count) + block, jnp.bfloat16),
            pltpu.VMEM((tp_count,) + block, jnp.bfloat16),
            pltpu.VMEM((tp_count,) + block, jnp.bfloat16),
            pltpu.VMEM((width, inner), jnp.bfloat16),
            pltpu.VMEM((width, inner), jnp.bfloat16),
            pltpu.VMEM((inner, width), jnp.bfloat16),
            pltpu.VMEM((side_count * own_rows, inner), jnp.bfloat16),
            dma((3,)),
            dma((side_count, tp_count)),
            dma((tp_count,)),
            dma((tp_count,)),
            dma((tp_count,)),
            dma((2, tp_count)),
            dma((half, tp_count)),
            dma((half, tp_count)),
            dma((tp_count,)),
            dma((tp_count,)),
            dma((tp_count,)),
            dma((tp_count,)),
        ],
        compiler_params=pltpu.CompilerParams(
            collective_id=0, has_side_effects=True, vmem_limit_bytes=58 * 2**20
        ),
        cost_estimate=pl.CostEstimate(
            flops=flops, bytes_accessed=6 * width * inner, transcendentals=0
        ),
        name="experts_exchange",
    )(
        normed,
        own_weight.reshape(side_count, tp_count, own_rows, 1),
        gate_weight,
        up_weight,
        down_weight,
    )


def dense_experts(
    stream, normed, gate_weight, up_weight, down_weight, expert_ids, numerators, experts_all
):
    weights = numerators.astype(jnp.float32)
    weights = weights / jnp.sum(weights, axis=1, keepdims=True)
    named = expert_ids[:, :, None] == jnp.arange(experts_all)[None, None, :]
    per_expert = jnp.sum(jnp.where(named, weights[:, :, None], 0.0), axis=1)
    all_weights = lax.all_gather(per_expert, ("side", "tp"), axis=0, tiled=True)
    me = lax.axis_index(("side", "tp"))
    own_weight = lax.dynamic_slice_in_dim(all_weights, me, 1, axis=1)
    if lax.axis_size("side") == 4:
        return stream + exchange_experts(normed, own_weight, gate_weight, up_weight, down_weight)
    rows = lax.all_gather(normed, ("side", "tp"), axis=0, tiled=True)
    gate_sum = jnp.dot(rows, gate_weight[0], preferred_element_type=jnp.float32)
    upward = jnp.dot(rows, up_weight[0], preferred_element_type=jnp.float32)
    hidden = (jax.nn.silu(gate_sum) * upward).astype(jnp.bfloat16)
    expert_out = jnp.dot(hidden, down_weight[0], preferred_element_type=jnp.float32)
    weighted = (expert_out * own_weight).astype(jnp.bfloat16)
    mixture = lax.psum_scatter(weighted, ("side", "tp"), scatter_dimension=0, tiled=True)
    return stream + mixture.astype(jnp.float32)


def local(
    queries,
    new_keys,
    new_values,
    cache_keys,
    cache_values,
    out_weight,
    residual,
    norm_gain,
    gate_weight,
    up_weight,
    down_weight,
    expert_ids,
    numerators,
):
    tp_count = lax.axis_size("tp")
    side_count = lax.axis_size("side")
    group_rows = queries.shape[0]
    local_heads = queries.shape[1] // HD
    head_kv = (lax.axis_index("tp") * local_heads + jnp.arange(local_heads)) // (H // KV)
    query_heads = queries.reshape(group_rows, local_heads, HD)
    score_scale = 1.0 / math.sqrt(HD)
    initial = (
        jnp.full((local_heads, group_rows), -1e30, jnp.float32),
        jnp.zeros((local_heads, group_rows), jnp.float32),
        jnp.zeros((local_heads, group_rows, HD), jnp.float32),
    )
    cache_both = lax.all_gather(
        jnp.concatenate([cache_keys[0], cache_values[0]], axis=1), "tp", axis=0, tiled=True
    )
    key_width = cache_keys.shape[2]
    key_piece = pick_heads(cache_both[:, :key_width], head_kv)
    value_piece = pick_heads(cache_both[:, key_width:], head_kv)
    scores = (
        jnp.einsum("rhd,nhd->hrn", query_heads, key_piece, preferred_element_type=jnp.float32)
        * score_scale
    )
    state_now = softmax_update(initial, scores, value_piece)
    own_keys = pick_heads(new_keys, head_kv)
    own_values = pick_heads(new_values, head_kv)
    scores = (
        jnp.einsum("rhd,nhd->hrn", query_heads, own_keys, preferred_element_type=jnp.float32)
        * score_scale
    )
    positions = jnp.arange(group_rows)
    visible = positions[None, :] <= positions[:, None]
    scores = jnp.where(visible[None], scores, -1e30)
    running, totals, context = softmax_update(state_now, scores, own_values)
    attended = (
        (context / totals[..., None])
        .transpose(1, 0, 2)
        .reshape(group_rows, local_heads * HD)
        .astype(jnp.bfloat16)
    )
    own_rows = residual.shape[0]
    attn_out = lax.psum_scatter(
        jnp.dot(attended, out_weight, preferred_element_type=jnp.float32).astype(jnp.bfloat16),
        "tp",
        scatter_dimension=0,
        tiled=True,
    ).astype(jnp.float32)
    stream = residual.astype(jnp.float32) + attn_out
    normed = (
        stream
        * lax.rsqrt(jnp.mean(stream * stream, axis=-1, keepdims=True) + 1e-06)
        * norm_gain.astype(jnp.float32)
    ).astype(jnp.bfloat16)
    experts_all = side_count * tp_count
    top_count = expert_ids.shape[1]
    copies = own_rows * top_count
    capacity = max(2, 2 * copies // experts_all)
    if capacity >= own_rows:
        return dense_experts(
            stream, normed, gate_weight, up_weight, down_weight, expert_ids, numerators, experts_all
        )
    flat_ids = expert_ids.reshape(copies)
    one_hot = (flat_ids[:, None] == jnp.arange(experts_all)[None, :]).astype(jnp.int32)
    earlier = jnp.cumsum(one_hot, axis=0) - one_hot
    slot_rank = jnp.sum(earlier * one_hot, axis=1)
    slot_index = flat_ids * capacity + slot_rank
    owners = jnp.arange(copies) // top_count
    outgoing = (
        jnp.zeros((experts_all * capacity, D), jnp.bfloat16).at[slot_index].set(normed[owners])
    )
    outgoing = outgoing.reshape(experts_all, capacity, D)
    buffer = lax.all_to_all(outgoing, ("side", "tp"), split_axis=0, concat_axis=0, tiled=True)
    buffer_shape = buffer.shape
    flat_rows = buffer.reshape(-1, D)
    gate_sum = jnp.dot(flat_rows, gate_weight[0], preferred_element_type=jnp.float32)
    upward = jnp.dot(flat_rows, up_weight[0], preferred_element_type=jnp.float32)
    hidden = (jax.nn.silu(gate_sum) * upward).astype(jnp.bfloat16)
    returned = lax.all_to_all(
        jnp.dot(hidden, down_weight[0], preferred_element_type=jnp.float32)
        .astype(jnp.bfloat16)
        .reshape(buffer_shape),
        ("side", "tp"),
        split_axis=0,
        concat_axis=0,
        tiled=True,
    )
    gathered = returned.reshape(experts_all * capacity, D)[slot_index]
    weights = numerators.astype(jnp.float32)
    weights = weights / jnp.sum(weights, axis=1, keepdims=True)
    mixture = jnp.sum(
        weights[:, :, None] * gathered.reshape(own_rows, top_count, D).astype(jnp.float32), axis=1
    )
    return stream + mixture


def solution(mesh):
    in_specs = (
        P(("replica", "side"), "tp"),
        P(("replica", "side"), None),
        P(("replica", "side"), None),
        P(("replica", "side"), "tp", None),
        P(("replica", "side"), "tp", None),
        P("tp", None),
        P(("replica", "side", "tp"), None),
        P(),
        P(("side", "tp"), None, None),
        P(("side", "tp"), None, None),
        P(("side", "tp"), None, None),
        P(("replica", "side", "tp"), None),
        P(("replica", "side", "tp"), None),
    )
    out_specs = P(("replica", "side", "tp"), None)
    return jax.shard_map(local, mesh=mesh, in_specs=in_specs, out_specs=out_specs, check_vma=False)
```

```python
import functools
import math

import jax
import jax.numpy as jnp
from jax import lax
from jax.experimental import pallas as pl
from jax.experimental.pallas import tpu as pltpu
from jax.sharding import PartitionSpec as P

D = 2048
H = 32
KV = 4
HD = 128
MESH = pl.DeviceIdType.MESH


def pick_heads(block_rows, head_kv):
    length_now = block_rows.shape[0]
    shaped = block_rows.reshape(length_now, KV, HD)
    return jnp.take(shaped, head_kv, axis=1)


def softmax_update(state_now, scores, values):
    running, totals, context = state_now
    highest = jnp.maximum(running, jnp.max(scores, axis=-1))
    factor = jnp.exp(running - highest)
    exponent = jnp.exp(scores - highest[..., None])
    totals = totals * factor + jnp.sum(exponent, axis=-1)
    context = context * factor[..., None] + jnp.einsum(
        "hrn,nhd->hrd", exponent.astype(jnp.bfloat16), values, preferred_element_type=jnp.float32
    )
    return (highest, totals, context)


def piece(length, most):
    return most if length % most == 0 else length


def near_first(at, step, count):
    found = jnp.int32(0)
    for place in range(count):
        order = sorted(range(count), key=lambda other: (abs(other - place), other))
        for turn in range(count):
            hit = jnp.logical_and(at == place, step == turn)
            found = found + jnp.where(hit, order[turn], 0)
    return found


def attend_kernel(
    tp_count, q_ref, new_k, new_v, cache_k, cache_v, out_hbm, residual_ref, gain_ref,
    stream_ref, normed_ref,
    keys, values, out_w, context, parts, from_below, from_above,
    load_sem, key_send, key_recv, value_send, value_recv, part_send, below_recv, above_recv,
):
    z = lax.axis_index("tp")
    top = tp_count - 1
    group_rows = q_ref.shape[0]
    local_heads = q_ref.shape[1] // HD
    own_rows = residual_ref.shape[0]
    cached = cache_k.shape[1]
    cache_len = cached * tp_count
    spot = pl.ds(pl.multiple_of(z * cached, cached), cached)

    def head_of(at):
        return pl.ds(pl.multiple_of(at * HD, HD), HD)

    tail = pl.ds(cache_len, group_rows)
    pairs = (
        (new_k.at[:, head_of(z)], keys.at[tail]),
        (new_v.at[:, head_of(z)], values.at[tail]),
        (cache_k.at[0, :, head_of(z)], keys.at[spot]),
        (cache_v.at[0, :, head_of(z)], values.at[spot]),
        (out_hbm, out_w),
    )
    loads = [
        pltpu.make_async_copy(source, target, load_sem.at[at])
        for at, (source, target) in enumerate(pairs)
    ]
    for load in loads:
        load.start()

    barrier = pltpu.get_barrier_semaphore()
    for step in range(1, tp_count):
        pl.semaphore_signal(
            barrier, inc=1, device_id={"tp": lax.rem(z + step, tp_count)}, device_id_type=MESH
        )
    pl.semaphore_wait(barrier, top)

    def give(source, target, at, start, send_sem, recv_sem):
        return pltpu.make_async_remote_copy(
            src_ref=source.at[0, :, head_of(at)],
            dst_ref=target.at[pl.ds(pl.multiple_of(start * cached, cached), cached)],
            send_sem=send_sem.at[at],
            recv_sem=recv_sem.at[start],
            device_id={"tp": at},
            device_id_type=MESH,
        )

    def gives(at, start):
        return (
            give(cache_k, keys, at, start, key_send, key_recv),
            give(cache_v, values, at, start, value_send, value_recv),
        )

    for step in range(1, tp_count):
        for copy in gives(lax.rem(z + step, tp_count), z):
            copy.start()

    def climb(at, target):
        return pltpu.make_async_remote_copy(
            src_ref=parts.at[at],
            dst_ref=from_below.at[at],
            send_sem=part_send.at[at],
            recv_sem=below_recv.at[at],
            device_id={"tp": target},
            device_id_type=MESH,
        )

    def descend(at, target):
        return pltpu.make_async_remote_copy(
            src_ref=parts.at[at],
            dst_ref=from_above.at[at],
            send_sem=part_send.at[at],
            recv_sem=above_recv.at[at],
            device_id={"tp": target},
            device_id_type=MESH,
        )

    above, below = jnp.minimum(z + 1, top), jnp.maximum(z - 1, 0)
    for load in loads:
        load.wait()
    for step in range(1, tp_count):
        peer = lax.rem(z + step, tp_count)
        for copy in gives(peer, peer):
            copy.wait_recv()

    score_scale = 1.0 / math.sqrt(HD)

    def project(step, carry):
        at = near_first(z, top - step, tp_count)
        own = pl.ds(pl.multiple_of(at * own_rows, own_rows), own_rows)
        shape = (own_rows, cache_len + group_rows)
        column = lax.broadcasted_iota(jnp.int32, shape, 1)
        position = lax.broadcasted_iota(jnp.int32, shape, 0) + at * own_rows
        visible = column <= position + cache_len
        for head in range(local_heads):
            lanes = pl.ds(head * HD, HD)
            scores = lax.dot_general(
                q_ref[own, lanes],
                keys[...],
                (((1,), (1,)), ((), ())),
                preferred_element_type=jnp.float32,
            )
            scores = jnp.where(visible, scores * score_scale, -1e30)
            exponent = jnp.exp(scores - jnp.max(scores, axis=-1, keepdims=True))
            totals = jnp.sum(exponent, axis=-1, keepdims=True)
            mixed = jnp.dot(
                exponent.astype(jnp.bfloat16), values[...], preferred_element_type=jnp.float32
            )
            context[:, lanes] = (mixed / totals).astype(jnp.bfloat16)
        parts[at] = jnp.dot(
            context[...], out_w[...], preferred_element_type=jnp.float32
        ).astype(jnp.bfloat16)

        @pl.when(jnp.logical_and(at > z, z == 0))
        def _():
            climb(at, above).start()

        @pl.when(jnp.logical_and(at < z, z == top))
        def _():
            descend(at, below).start()

        return carry

    lax.fori_loop(0, tp_count, project, 0)

    def add_to(at, arrived):
        parts[at] = (
            parts[at].astype(jnp.float32) + arrived[at].astype(jnp.float32)
        ).astype(jnp.bfloat16)

    def hand_on(step, carry):
        at = near_first(z, top - step, tp_count)

        @pl.when(jnp.logical_and(at > z, z > 0))
        def _():
            climb(at, above).wait_recv()
            add_to(at, from_below)
            climb(at, above).start()

        @pl.when(jnp.logical_and(at < z, z < top))
        def _():
            descend(at, below).wait_recv()
            add_to(at, from_above)
            descend(at, below).start()

        return carry

    lax.fori_loop(0, top, hand_on, 0)
    stream_ref[...] = residual_ref[...].astype(jnp.float32) + parts[z].astype(jnp.float32)

    @pl.when(z > 0)
    def _():
        climb(z, above).wait_recv()
        stream_ref[...] += from_below[z].astype(jnp.float32)

    @pl.when(z < top)
    def _():
        descend(z, below).wait_recv()
        stream_ref[...] += from_above[z].astype(jnp.float32)

    stream = stream_ref[...]
    normed_ref[...] = (
        stream
        * lax.rsqrt(jnp.mean(stream * stream, axis=-1, keepdims=True) + 1e-06)
        * gain_ref[...].astype(jnp.float32)
    ).astype(jnp.bfloat16)

    for step in range(1, tp_count):
        peer = lax.rem(z + step, tp_count)
        for copy in gives(peer, z):
            copy.wait_send()

    def drain(at, carry):
        pl.when(at > z)(climb(at, above).wait_send)
        pl.when(at < z)(descend(at, below).wait_send)
        return carry

    lax.fori_loop(0, tp_count, drain, 0)


def attend_rows(
    queries, new_keys, new_values, cache_keys, cache_values, out_weight, residual, norm_gain
):
    tp_count = lax.axis_size("tp")
    group_rows, head_columns = queries.shape
    own_rows, width = residual.shape
    key_rows = cache_keys.shape[1] * tp_count + group_rows
    dma = pltpu.SemaphoreType.DMA
    block = (own_rows, width)
    in_vmem = pl.BlockSpec(memory_space=pltpu.VMEM)
    in_any = pl.BlockSpec(memory_space=pl.ANY)
    return pl.pallas_call(
        functools.partial(attend_kernel, tp_count),
        out_shape=(
            jax.ShapeDtypeStruct(block, jnp.float32),
            jax.ShapeDtypeStruct(block, jnp.bfloat16),
        ),
        in_specs=[in_vmem] + [in_any] * 5 + [in_vmem] * 2,
        out_specs=(in_vmem, in_vmem),
        scratch_shapes=[
            pltpu.VMEM((key_rows, HD), jnp.bfloat16),
            pltpu.VMEM((key_rows, HD), jnp.bfloat16),
            pltpu.VMEM((head_columns, width), jnp.bfloat16),
            pltpu.VMEM((own_rows, head_columns), jnp.bfloat16),
            pltpu.VMEM((tp_count,) + block, jnp.bfloat16),
            pltpu.VMEM((tp_count,) + block, jnp.bfloat16),
            pltpu.VMEM((tp_count,) + block, jnp.bfloat16),
            dma((5,)),
        ]
        + [dma((tp_count,))] * 7,
        compiler_params=pltpu.CompilerParams(
            collective_id=1, has_side_effects=True, vmem_limit_bytes=48 * 2**20
        ),
        cost_estimate=pl.CostEstimate(
            flops=4 * group_rows * key_rows * head_columns + 2 * group_rows * head_columns * width,
            bytes_accessed=2 * head_columns * width,
            transcendentals=0,
        ),
        name="attend_rows",
    )(
        queries,
        new_keys,
        new_values,
        cache_keys,
        cache_values,
        out_weight,
        residual,
        norm_gain.reshape(1, width),
    )


def experts_kernel(
    side_count, tp_count, own_ref, weight_ref, gate_hbm, up_hbm, down_hbm, mix_ref,
    rows, parts, from_core, from_y, from_z, gate, up, down, hidden,
    load_sem, row_recv, up_send, down_send, y_send, core_send,
    core1_send, core1_recv, y1_send, y1_recv, z1_send, z1_recv,
):
    side, z = lax.axis_index("side"), lax.axis_index("tp")
    y, core = side // 2, side % 2
    other_y, other_core = side + 2 - 4 * y, side + 1 - 2 * core
    far_core = other_y + 1 - 2 * core
    own_rows, width = own_ref.shape
    spare = weight_ref.shape[1]
    inner = gate.shape[1]
    me = lax.axis_index(("side", "tp"))
    loads = [
        pltpu.make_async_copy(source.at[0], target, load_sem.at[at])
        for at, (source, target) in enumerate(((gate_hbm, gate), (up_hbm, up), (down_hbm, down)))
    ]
    for load in loads:
        load.start()

    barrier = pltpu.get_barrier_semaphore()
    for step in range(1, tp_count):
        pl.semaphore_signal(
            barrier, inc=1, device_id={"tp": lax.rem(z + step, tp_count)}, device_id_type=MESH
        )
    for target in (other_y, other_core):
        pl.semaphore_signal(barrier, inc=1, device_id={"side": target}, device_id_type=MESH)
    pl.semaphore_wait(barrier, tp_count + 1)

    def send_row(at_side, at_z, send_sem, target):
        return pltpu.make_async_remote_copy(
            src_ref=rows.at[at_side, at_z],
            dst_ref=rows.at[at_side, at_z],
            send_sem=send_sem,
            recv_sem=row_recv.at[at_side, at_z],
            device_id=target,
            device_id_type=MESH,
        )

    def wait_row(at_side, at_z):
        send_row(at_side, at_z, up_send.at[at_z], {"side": other_core}).wait_recv()

    def line_sends(at_z):
        return (
            (
                jnp.logical_and(at_z <= z, z < tp_count - 1),
                send_row(side, at_z, up_send.at[at_z], {"tp": jnp.minimum(z + 1, tp_count - 1)}),
            ),
            (
                jnp.logical_and(at_z >= z, z > 0),
                send_row(side, at_z, down_send.at[at_z], {"tp": jnp.maximum(z - 1, 0)}),
            ),
        )

    def side_sends(at_z):
        return (
            send_row(side, at_z, y_send.at[at_z], {"side": other_y}),
            send_row(side, at_z, core_send.at[0, at_z], {"side": other_core}),
        )

    def pass_on(at_z):
        return send_row(other_y, at_z, core_send.at[1, at_z], {"side": other_core})

    def spread(at_z):
        for condition, copy in line_sends(at_z):
            pl.when(condition)(copy.start)
        for copy in side_sends(at_z):
            copy.start()

    def to_core(at_y, at_z):
        return pltpu.make_async_remote_copy(
            src_ref=parts.at[2 * at_y + 1 - core, at_z],
            dst_ref=from_core.at[at_y, at_z],
            send_sem=core1_send.at[at_y, at_z],
            recv_sem=core1_recv.at[at_y, at_z],
            device_id={"side": other_core},
            device_id_type=MESH,
        )

    def to_y(at_z):
        return pltpu.make_async_remote_copy(
            src_ref=parts.at[other_y, at_z],
            dst_ref=from_y.at[at_z],
            send_sem=y1_send.at[at_z],
            recv_sem=y1_recv.at[at_z],
            device_id={"side": other_y},
            device_id_type=MESH,
        )

    def to_line(at_z, slot, target):
        return pltpu.make_async_remote_copy(
            src_ref=parts.at[side, at_z],
            dst_ref=from_z.at[slot],
            send_sem=z1_send.at[at_z],
            recv_sem=z1_recv.at[slot],
            device_id={"tp": target},
            device_id_type=MESH,
        )

    def add_to_part(at_side, at_z, arrived):
        parts[at_side, at_z] = (
            parts[at_side, at_z].astype(jnp.float32) + arrived[...].astype(jnp.float32)
        ).astype(jnp.bfloat16)

    rows[side, z, :, :width] = own_ref[...]
    rows[side, z, :, width:] = weight_ref[...]
    spread(z)
    for load in loads:
        load.wait()

    def forward(step, carry):
        at_z = near_first(z, step, tp_count)

        @pl.when(step + 1 < tp_count)
        def _():
            next_z = near_first(z, step + 1, tp_count)
            wait_row(side, next_z)
            spread(next_z)

        wait_row(other_y, at_z)
        pass_on(at_z).start()
        wait_row(other_core, at_z)
        wait_row(far_core, at_z)
        count = side_count * own_rows
        block = piece(inner, 256)

        def hide(at, carry):
            columns = pl.ds(pl.multiple_of(at * block, block), block)
            taken = rows[:, at_z, :, :width].reshape(count, width)
            gate_sum = jnp.dot(taken, gate[:, columns], preferred_element_type=jnp.float32)
            upward = jnp.dot(taken, up[:, columns], preferred_element_type=jnp.float32)
            hidden[:, columns] = (gate_sum / (1.0 + jnp.exp(-gate_sum)) * upward).astype(
                jnp.bfloat16
            )
            return carry

        lax.fori_loop(0, inner // block, hide, 0)
        out_block = piece(width, 512)

        def show(at, carry):
            columns = pl.ds(pl.multiple_of(at * out_block, out_block), out_block)
            out = jnp.dot(hidden[...], down[:, columns], preferred_element_type=jnp.float32)
            listed = rows[:, at_z, :, width:].reshape(count, spare).astype(jnp.float32)
            lane = lax.broadcasted_iota(jnp.int32, (count, spare), 1)
            mine = jnp.logical_or(lane == me, lane == me + side_count * tp_count)
            scale = jnp.sum(jnp.where(mine, listed, 0.0), axis=1, keepdims=True)
            parts[:, at_z, :, columns] = (
                (out * scale).astype(jnp.bfloat16).reshape(side_count, own_rows, out_block)
            )
            return carry

        lax.fori_loop(0, width // out_block, show, 0)
        for at_y in range(side_count // 2):
            to_core(at_y, at_z).start()
        return carry

    lax.fori_loop(0, tp_count, forward, 0)

    def back_y(step, carry):
        at_z = near_first(z, tp_count - 1 - step, tp_count)
        to_core(1 - y, at_z).wait_recv()
        add_to_part(other_y, at_z, from_core.at[1 - y, at_z])
        to_y(at_z).start()
        to_core(y, at_z).wait_recv()
        add_to_part(side, at_z, from_core.at[y, at_z])
        return carry

    lax.fori_loop(0, tp_count, back_y, 0)

    def back_z(step, carry):
        at_z = near_first(z, tp_count - 1 - step, tp_count)
        to_y(at_z).wait_recv()
        add_to_part(side, at_z, from_y.at[at_z])
        to_line(at_z, z, at_z).start()
        return carry

    lax.fori_loop(0, tp_count - 1, back_z, 0)
    to_y(z).wait_recv()
    mix_ref[...] = parts[side, z].astype(jnp.float32) + from_y[z].astype(jnp.float32)

    def collect(step, carry):
        at_z = near_first(z, step, tp_count)
        to_line(at_z, at_z, at_z).wait_recv()
        mix_ref[...] += from_z[at_z].astype(jnp.float32)
        return carry

    lax.fori_loop(1, tp_count, collect, 0)

    def drain(at_z, carry):
        for condition, copy in line_sends(at_z):
            pl.when(condition)(copy.wait_send)
        for copy in side_sends(at_z):
            copy.wait_send()
        pass_on(at_z).wait_send()
        for at_y in range(side_count // 2):
            to_core(at_y, at_z).wait_send()
        to_y(at_z).wait_send()
        pl.when(at_z != z)(to_line(at_z, z, at_z).wait_send)
        return carry

    lax.fori_loop(0, tp_count, drain, 0)


def exchange_experts(normed, listed, gate_weight, up_weight, down_weight):
    side_count, tp_count = lax.axis_size("side"), lax.axis_size("tp")
    own_rows, width = normed.shape
    inner = gate_weight.shape[2]
    half = side_count // 2
    dma = pltpu.SemaphoreType.DMA
    block = (own_rows, width)
    flops = 6 * side_count * tp_count * own_rows * width * inner
    return pl.pallas_call(
        functools.partial(experts_kernel, side_count, tp_count),
        out_shape=jax.ShapeDtypeStruct(block, jnp.float32),
        in_specs=[pl.BlockSpec(memory_space=pltpu.VMEM)] * 2
        + [pl.BlockSpec(memory_space=pl.ANY)] * 3,
        out_specs=pl.BlockSpec(memory_space=pltpu.VMEM),
        scratch_shapes=[
            pltpu.VMEM((side_count, tp_count, own_rows, width + listed.shape[1]), jnp.bfloat16),
            pltpu.VMEM((side_count, tp_count) + block, jnp.bfloat16),
            pltpu.VMEM((half, tp_count) + block, jnp.bfloat16),
            pltpu.VMEM((tp_count,) + block, jnp.bfloat16),
            pltpu.VMEM((tp_count,) + block, jnp.bfloat16),
            pltpu.VMEM((width, inner), jnp.bfloat16),
            pltpu.VMEM((width, inner), jnp.bfloat16),
            pltpu.VMEM((inner, width), jnp.bfloat16),
            pltpu.VMEM((side_count * own_rows, inner), jnp.bfloat16),
            dma((3,)),
            dma((side_count, tp_count)),
            dma((tp_count,)),
            dma((tp_count,)),
            dma((tp_count,)),
            dma((2, tp_count)),
            dma((half, tp_count)),
            dma((half, tp_count)),
            dma((tp_count,)),
            dma((tp_count,)),
            dma((tp_count,)),
            dma((tp_count,)),
        ],
        compiler_params=pltpu.CompilerParams(
            collective_id=0, has_side_effects=True, vmem_limit_bytes=58 * 2**20
        ),
        cost_estimate=pl.CostEstimate(
            flops=flops, bytes_accessed=6 * width * inner, transcendentals=0
        ),
        name="experts_exchange",
    )(
        normed,
        listed,
        gate_weight,
        up_weight,
        down_weight,
    )


def dense_experts(
    stream, normed, gate_weight, up_weight, down_weight, expert_ids, numerators, experts_all
):
    weights = numerators.astype(jnp.float32)
    weights = weights / jnp.sum(weights, axis=1, keepdims=True)
    named = expert_ids[:, :, None] == jnp.arange(experts_all)[None, None, :]
    per_expert = jnp.sum(jnp.where(named, weights[:, :, None], 0.0), axis=1)
    if lax.axis_size("side") == 4 and 2 * experts_all <= 128:
        high = lax.reduce_precision(per_expert, 8, 7)
        spare = jnp.zeros((stream.shape[0], 128 - 2 * experts_all), jnp.float32)
        listed = jnp.concatenate([high, per_expert - high, spare], axis=1).astype(jnp.bfloat16)
        return stream + exchange_experts(normed, listed, gate_weight, up_weight, down_weight)
    all_weights = lax.all_gather(per_expert, ("side", "tp"), axis=0, tiled=True)
    me = lax.axis_index(("side", "tp"))
    own_weight = lax.dynamic_slice_in_dim(all_weights, me, 1, axis=1)
    rows = lax.all_gather(normed, ("side", "tp"), axis=0, tiled=True)
    gate_sum = jnp.dot(rows, gate_weight[0], preferred_element_type=jnp.float32)
    upward = jnp.dot(rows, up_weight[0], preferred_element_type=jnp.float32)
    hidden = (jax.nn.silu(gate_sum) * upward).astype(jnp.bfloat16)
    expert_out = jnp.dot(hidden, down_weight[0], preferred_element_type=jnp.float32)
    weighted = (expert_out * own_weight).astype(jnp.bfloat16)
    mixture = lax.psum_scatter(weighted, ("side", "tp"), scatter_dimension=0, tiled=True)
    return stream + mixture.astype(jnp.float32)


def attend_plain(
    queries, new_keys, new_values, cache_keys, cache_values, out_weight, residual, norm_gain
):
    group_rows = queries.shape[0]
    local_heads = queries.shape[1] // HD
    head_kv = (lax.axis_index("tp") * local_heads + jnp.arange(local_heads)) // (H // KV)
    query_heads = queries.reshape(group_rows, local_heads, HD)
    score_scale = 1.0 / math.sqrt(HD)
    initial = (
        jnp.full((local_heads, group_rows), -1e30, jnp.float32),
        jnp.zeros((local_heads, group_rows), jnp.float32),
        jnp.zeros((local_heads, group_rows, HD), jnp.float32),
    )
    cache_both = lax.all_gather(
        jnp.concatenate([cache_keys[0], cache_values[0]], axis=1), "tp", axis=0, tiled=True
    )
    key_width = cache_keys.shape[2]
    key_piece = pick_heads(cache_both[:, :key_width], head_kv)
    value_piece = pick_heads(cache_both[:, key_width:], head_kv)
    scores = (
        jnp.einsum("rhd,nhd->hrn", query_heads, key_piece, preferred_element_type=jnp.float32)
        * score_scale
    )
    state_now = softmax_update(initial, scores, value_piece)
    own_keys = pick_heads(new_keys, head_kv)
    own_values = pick_heads(new_values, head_kv)
    scores = (
        jnp.einsum("rhd,nhd->hrn", query_heads, own_keys, preferred_element_type=jnp.float32)
        * score_scale
    )
    positions = jnp.arange(group_rows)
    visible = positions[None, :] <= positions[:, None]
    scores = jnp.where(visible[None], scores, -1e30)
    running, totals, context = softmax_update(state_now, scores, own_values)
    attended = (
        (context / totals[..., None])
        .transpose(1, 0, 2)
        .reshape(group_rows, local_heads * HD)
        .astype(jnp.bfloat16)
    )
    own_rows = residual.shape[0]
    attn_out = lax.psum_scatter(
        jnp.dot(attended, out_weight, preferred_element_type=jnp.float32).astype(jnp.bfloat16),
        "tp",
        scatter_dimension=0,
        tiled=True,
    ).astype(jnp.float32)
    stream = residual.astype(jnp.float32) + attn_out
    normed = (
        stream
        * lax.rsqrt(jnp.mean(stream * stream, axis=-1, keepdims=True) + 1e-06)
        * norm_gain.astype(jnp.float32)
    ).astype(jnp.bfloat16)
    return stream, normed


def local(
    queries,
    new_keys,
    new_values,
    cache_keys,
    cache_values,
    out_weight,
    residual,
    norm_gain,
    gate_weight,
    up_weight,
    down_weight,
    expert_ids,
    numerators,
):
    tp_count = lax.axis_size("tp")
    side_count = lax.axis_size("side")
    own_rows = residual.shape[0]
    attend = attend_rows if tp_count == KV else attend_plain
    stream, normed = attend(
        queries, new_keys, new_values, cache_keys, cache_values, out_weight, residual, norm_gain
    )
    experts_all = side_count * tp_count
    top_count = expert_ids.shape[1]
    copies = own_rows * top_count
    capacity = max(2, 2 * copies // experts_all)
    if capacity >= own_rows:
        return dense_experts(
            stream, normed, gate_weight, up_weight, down_weight, expert_ids, numerators, experts_all
        )
    flat_ids = expert_ids.reshape(copies)
    one_hot = (flat_ids[:, None] == jnp.arange(experts_all)[None, :]).astype(jnp.int32)
    earlier = jnp.cumsum(one_hot, axis=0) - one_hot
    slot_rank = jnp.sum(earlier * one_hot, axis=1)
    slot_index = flat_ids * capacity + slot_rank
    owners = jnp.arange(copies) // top_count
    outgoing = (
        jnp.zeros((experts_all * capacity, D), jnp.bfloat16).at[slot_index].set(normed[owners])
    )
    outgoing = outgoing.reshape(experts_all, capacity, D)
    buffer = lax.all_to_all(outgoing, ("side", "tp"), split_axis=0, concat_axis=0, tiled=True)
    buffer_shape = buffer.shape
    flat_rows = buffer.reshape(-1, D)
    gate_sum = jnp.dot(flat_rows, gate_weight[0], preferred_element_type=jnp.float32)
    upward = jnp.dot(flat_rows, up_weight[0], preferred_element_type=jnp.float32)
    hidden = (jax.nn.silu(gate_sum) * upward).astype(jnp.bfloat16)
    returned = lax.all_to_all(
        jnp.dot(hidden, down_weight[0], preferred_element_type=jnp.float32)
        .astype(jnp.bfloat16)
        .reshape(buffer_shape),
        ("side", "tp"),
        split_axis=0,
        concat_axis=0,
        tiled=True,
    )
    gathered = returned.reshape(experts_all * capacity, D)[slot_index]
    weights = numerators.astype(jnp.float32)
    weights = weights / jnp.sum(weights, axis=1, keepdims=True)
    mixture = jnp.sum(
        weights[:, :, None] * gathered.reshape(own_rows, top_count, D).astype(jnp.float32), axis=1
    )
    return stream + mixture


def solution(mesh):
    in_specs = (
        P(("replica", "side"), "tp"),
        P(("replica", "side"), None),
        P(("replica", "side"), None),
        P(("replica", "side"), "tp", None),
        P(("replica", "side"), "tp", None),
        P("tp", None),
        P(("replica", "side", "tp"), None),
        P(),
        P(("side", "tp"), None, None),
        P(("side", "tp"), None, None),
        P(("side", "tp"), None, None),
        P(("replica", "side", "tp"), None),
        P(("replica", "side", "tp"), None),
    )
    out_specs = P(("replica", "side", "tp"), None)
    return jax.shard_map(local, mesh=mesh, in_specs=in_specs, out_specs=out_specs, check_vma=False)
```

```python
import functools
import math

import jax
import jax.numpy as jnp
from jax import lax
from jax.experimental import pallas as pl
from jax.experimental.pallas import tpu as pltpu
from jax.sharding import PartitionSpec as P

D = 2048
H = 32
KV = 4
HD = 128
MESH = pl.DeviceIdType.MESH


def pick_heads(block_rows, head_kv):
    length_now = block_rows.shape[0]
    shaped = block_rows.reshape(length_now, KV, HD)
    return jnp.take(shaped, head_kv, axis=1)


def softmax_update(state_now, scores, values):
    running, totals, context = state_now
    highest = jnp.maximum(running, jnp.max(scores, axis=-1))
    factor = jnp.exp(running - highest)
    exponent = jnp.exp(scores - highest[..., None])
    totals = totals * factor + jnp.sum(exponent, axis=-1)
    context = context * factor[..., None] + jnp.einsum(
        "hrn,nhd->hrd", exponent.astype(jnp.bfloat16), values, preferred_element_type=jnp.float32
    )
    return (highest, totals, context)


def piece(length, most):
    return most if length % most == 0 else length


def near_first(at, step, count):
    found = jnp.int32(0)
    for place in range(count):
        order = sorted(range(count), key=lambda other: (abs(other - place), other))
        for turn in range(count):
            hit = jnp.logical_and(at == place, step == turn)
            found = found + jnp.where(hit, order[turn], 0)
    return found


def attend_kernel(
    tp_count, q_ref, new_k, new_v, cache_k, cache_v, out_hbm, residual_ref, gain_ref,
    stream_ref, normed_ref,
    keys, values, out_w, context, parts, from_below, from_above,
    load_sem, key_send, key_recv, value_send, value_recv, part_send, below_recv, above_recv,
):
    z = lax.axis_index("tp")
    top = tp_count - 1
    group_rows = q_ref.shape[0]
    local_heads = q_ref.shape[1] // HD
    own_rows = residual_ref.shape[0]
    cached = cache_k.shape[1]
    cache_len = cached * tp_count
    spot = pl.ds(pl.multiple_of(z * cached, cached), cached)

    def head_of(at):
        return pl.ds(pl.multiple_of(at * HD, HD), HD)

    tail = pl.ds(cache_len, group_rows)
    pairs = (
        (new_k.at[:, head_of(z)], keys.at[tail]),
        (new_v.at[:, head_of(z)], values.at[tail]),
        (cache_k.at[0, :, head_of(z)], keys.at[spot]),
        (cache_v.at[0, :, head_of(z)], values.at[spot]),
        (out_hbm, out_w),
    )
    loads = [
        pltpu.make_async_copy(source, target, load_sem.at[at])
        for at, (source, target) in enumerate(pairs)
    ]
    for load in loads:
        load.start()

    barrier = pltpu.get_barrier_semaphore()
    for step in range(1, tp_count):
        pl.semaphore_signal(
            barrier, inc=1, device_id={"tp": lax.rem(z + step, tp_count)}, device_id_type=MESH
        )
    pl.semaphore_wait(barrier, top)

    def give(source, target, at, start, send_sem, recv_sem):
        return pltpu.make_async_remote_copy(
            src_ref=source.at[0, :, head_of(at)],
            dst_ref=target.at[pl.ds(pl.multiple_of(start * cached, cached), cached)],
            send_sem=send_sem.at[at],
            recv_sem=recv_sem.at[start],
            device_id={"tp": at},
            device_id_type=MESH,
        )

    def gives(at, start):
        return (
            give(cache_k, keys, at, start, key_send, key_recv),
            give(cache_v, values, at, start, value_send, value_recv),
        )

    for step in range(1, tp_count):
        for copy in gives(lax.rem(z + step, tp_count), z):
            copy.start()

    def climb(at, target):
        return pltpu.make_async_remote_copy(
            src_ref=parts.at[at],
            dst_ref=from_below.at[at],
            send_sem=part_send.at[at],
            recv_sem=below_recv.at[at],
            device_id={"tp": target},
            device_id_type=MESH,
        )

    def descend(at, target):
        return pltpu.make_async_remote_copy(
            src_ref=parts.at[at],
            dst_ref=from_above.at[at],
            send_sem=part_send.at[at],
            recv_sem=above_recv.at[at],
            device_id={"tp": target},
            device_id_type=MESH,
        )

    above, below = jnp.minimum(z + 1, top), jnp.maximum(z - 1, 0)
    for load in loads:
        load.wait()
    for step in range(1, tp_count):
        peer = lax.rem(z + step, tp_count)
        for copy in gives(peer, peer):
            copy.wait_recv()

    score_scale = 1.0 / math.sqrt(HD)

    def project(step, carry):
        at = near_first(z, top - step, tp_count)
        own = pl.ds(pl.multiple_of(at * own_rows, own_rows), own_rows)
        shape = (own_rows, cache_len + group_rows)
        column = lax.broadcasted_iota(jnp.int32, shape, 1)
        position = lax.broadcasted_iota(jnp.int32, shape, 0) + at * own_rows
        visible = column <= position + cache_len
        for head in range(local_heads):
            lanes = pl.ds(head * HD, HD)
            scores = lax.dot_general(
                q_ref[own, lanes],
                keys[...],
                (((1,), (1,)), ((), ())),
                preferred_element_type=jnp.float32,
            )
            scores = jnp.where(visible, scores * score_scale, -1e30)
            exponent = jnp.exp(scores - jnp.max(scores, axis=-1, keepdims=True))
            totals = jnp.sum(exponent, axis=-1, keepdims=True)
            mixed = jnp.dot(
                exponent.astype(jnp.bfloat16), values[...], preferred_element_type=jnp.float32
            )
            context[:, lanes] = (mixed / totals).astype(jnp.bfloat16)
        parts[at] = jnp.dot(
            context[...], out_w[...], preferred_element_type=jnp.float32
        ).astype(jnp.bfloat16)

        @pl.when(jnp.logical_and(at > z, z == 0))
        def _():
            climb(at, above).start()

        @pl.when(jnp.logical_and(at < z, z == top))
        def _():
            descend(at, below).start()

        return carry

    lax.fori_loop(0, tp_count, project, 0)

    def add_to(at, arrived):
        parts[at] = (
            parts[at].astype(jnp.float32) + arrived[at].astype(jnp.float32)
        ).astype(jnp.bfloat16)

    def hand_on(step, carry):
        at = near_first(z, top - step, tp_count)

        @pl.when(jnp.logical_and(at > z, z > 0))
        def _():
            climb(at, above).wait_recv()
            add_to(at, from_below)
            climb(at, above).start()

        @pl.when(jnp.logical_and(at < z, z < top))
        def _():
            descend(at, below).wait_recv()
            add_to(at, from_above)
            descend(at, below).start()

        return carry

    lax.fori_loop(0, top, hand_on, 0)
    stream_ref[...] = residual_ref[...].astype(jnp.float32) + parts[z].astype(jnp.float32)

    @pl.when(z > 0)
    def _():
        climb(z, above).wait_recv()
        stream_ref[...] += from_below[z].astype(jnp.float32)

    @pl.when(z < top)
    def _():
        descend(z, below).wait_recv()
        stream_ref[...] += from_above[z].astype(jnp.float32)

    stream = stream_ref[...]
    normed_ref[...] = (
        stream
        * lax.rsqrt(jnp.mean(stream * stream, axis=-1, keepdims=True) + 1e-06)
        * gain_ref[...].astype(jnp.float32)
    ).astype(jnp.bfloat16)

    for step in range(1, tp_count):
        peer = lax.rem(z + step, tp_count)
        for copy in gives(peer, z):
            copy.wait_send()

    def drain(at, carry):
        pl.when(at > z)(climb(at, above).wait_send)
        pl.when(at < z)(descend(at, below).wait_send)
        return carry

    lax.fori_loop(0, tp_count, drain, 0)


def attend_rows(
    queries, new_keys, new_values, cache_keys, cache_values, out_weight, residual, norm_gain
):
    tp_count = lax.axis_size("tp")
    group_rows, head_columns = queries.shape
    own_rows, width = residual.shape
    key_rows = cache_keys.shape[1] * tp_count + group_rows
    dma = pltpu.SemaphoreType.DMA
    block = (own_rows, width)
    in_vmem = pl.BlockSpec(memory_space=pltpu.VMEM)
    in_any = pl.BlockSpec(memory_space=pltpu.HBM)
    return pl.pallas_call(
        functools.partial(attend_kernel, tp_count),
        out_shape=(
            jax.ShapeDtypeStruct(block, jnp.float32),
            jax.ShapeDtypeStruct(block, jnp.bfloat16),
        ),
        in_specs=[in_vmem] + [in_any] * 5 + [in_vmem] * 2,
        out_specs=(in_vmem, in_vmem),
        scratch_shapes=[
            pltpu.VMEM((key_rows, HD), jnp.bfloat16),
            pltpu.VMEM((key_rows, HD), jnp.bfloat16),
            pltpu.VMEM((head_columns, width), jnp.bfloat16),
            pltpu.VMEM((own_rows, head_columns), jnp.bfloat16),
            pltpu.VMEM((tp_count,) + block, jnp.bfloat16),
            pltpu.VMEM((tp_count,) + block, jnp.bfloat16),
            pltpu.VMEM((tp_count,) + block, jnp.bfloat16),
            dma((5,)),
        ]
        + [dma((tp_count,))] * 7,
        compiler_params=pltpu.CompilerParams(
            collective_id=1, has_side_effects=True, vmem_limit_bytes=58 * 2**20
        ),
        cost_estimate=pl.CostEstimate(
            flops=4 * group_rows * key_rows * head_columns + 2 * group_rows * head_columns * width,
            bytes_accessed=2 * head_columns * width,
            transcendentals=0,
        ),
        name="attend_rows",
    )(
        queries,
        new_keys,
        new_values,
        cache_keys,
        cache_values,
        out_weight,
        residual,
        norm_gain.reshape(1, width),
    )


def experts_kernel(
    side_count, tp_count, own_ref, weight_ref, gate_hbm, up_hbm, down_hbm, mix_ref,
    rows, parts, from_core, from_y, from_z, gate, up, down, hidden,
    load_sem, row_recv, up_send, down_send, y_send, core_send,
    core1_send, core1_recv, y1_send, y1_recv, z1_send, z1_recv,
):
    side, z = lax.axis_index("side"), lax.axis_index("tp")
    y, core = side // 2, side % 2
    other_y, other_core = side + 2 - 4 * y, side + 1 - 2 * core
    far_core = other_y + 1 - 2 * core
    own_rows, width = own_ref.shape
    spare = weight_ref.shape[1]
    inner = gate.shape[1]
    me = lax.axis_index(("side", "tp"))
    loads = [
        pltpu.make_async_copy(source.at[0], target, load_sem.at[at])
        for at, (source, target) in enumerate(((gate_hbm, gate), (up_hbm, up), (down_hbm, down)))
    ]
    for load in loads:
        load.start()

    barrier = pltpu.get_barrier_semaphore()
    for step in range(1, tp_count):
        pl.semaphore_signal(
            barrier, inc=1, device_id={"tp": lax.rem(z + step, tp_count)}, device_id_type=MESH
        )
    for target in (other_y, other_core):
        pl.semaphore_signal(barrier, inc=1, device_id={"side": target}, device_id_type=MESH)
    pl.semaphore_wait(barrier, tp_count + 1)

    def send_row(at_side, at_z, send_sem, target):
        return pltpu.make_async_remote_copy(
            src_ref=rows.at[at_side, at_z],
            dst_ref=rows.at[at_side, at_z],
            send_sem=send_sem,
            recv_sem=row_recv.at[at_side, at_z],
            device_id=target,
            device_id_type=MESH,
        )

    def wait_row(at_side, at_z):
        send_row(at_side, at_z, up_send.at[at_z], {"side": other_core}).wait_recv()

    def line_sends(at_z):
        return (
            (
                jnp.logical_and(at_z <= z, z < tp_count - 1),
                send_row(side, at_z, up_send.at[at_z], {"tp": jnp.minimum(z + 1, tp_count - 1)}),
            ),
            (
                jnp.logical_and(at_z >= z, z > 0),
                send_row(side, at_z, down_send.at[at_z], {"tp": jnp.maximum(z - 1, 0)}),
            ),
        )

    def side_sends(at_z):
        return (
            send_row(side, at_z, y_send.at[at_z], {"side": other_y}),
            send_row(side, at_z, core_send.at[0, at_z], {"side": other_core}),
        )

    def pass_on(at_z):
        return send_row(other_y, at_z, core_send.at[1, at_z], {"side": other_core})

    def spread(at_z):
        for condition, copy in line_sends(at_z):
            pl.when(condition)(copy.start)
        for copy in side_sends(at_z):
            copy.start()

    def to_core(at_y, at_z):
        return pltpu.make_async_remote_copy(
            src_ref=parts.at[2 * at_y + 1 - core, at_z],
            dst_ref=from_core.at[at_y, at_z],
            send_sem=core1_send.at[at_y, at_z],
            recv_sem=core1_recv.at[at_y, at_z],
            device_id={"side": other_core},
            device_id_type=MESH,
        )

    def to_y(at_z):
        return pltpu.make_async_remote_copy(
            src_ref=parts.at[other_y, at_z],
            dst_ref=from_y.at[at_z],
            send_sem=y1_send.at[at_z],
            recv_sem=y1_recv.at[at_z],
            device_id={"side": other_y},
            device_id_type=MESH,
        )

    def to_line(at_z, slot, target):
        return pltpu.make_async_remote_copy(
            src_ref=parts.at[side, at_z],
            dst_ref=from_z.at[slot],
            send_sem=z1_send.at[at_z],
            recv_sem=z1_recv.at[slot],
            device_id={"tp": target},
            device_id_type=MESH,
        )

    def add_to_part(at_side, at_z, arrived):
        parts[at_side, at_z] = (
            parts[at_side, at_z].astype(jnp.float32) + arrived[...].astype(jnp.float32)
        ).astype(jnp.bfloat16)

    rows[side, z, :, :width] = own_ref[...]
    rows[side, z, :, width:] = weight_ref[...]
    spread(z)
    inside = jnp.logical_and(z > 0, z < tp_count - 1)

    @pl.when(inside)
    def _():
        next_z = near_first(z, 1, tp_count)
        wait_row(side, next_z)
        spread(next_z)

    for load in loads:
        load.wait()

    def back_y(at_z):
        to_core(1 - y, at_z).wait_recv()
        add_to_part(other_y, at_z, from_core.at[1 - y, at_z])
        to_y(at_z).start()
        to_core(y, at_z).wait_recv()
        add_to_part(side, at_z, from_core.at[y, at_z])

    def return_order(step):
        turn = jnp.where(step == 0, tp_count - 2, tp_count - 1 - step)
        return near_first(z, jnp.where(step == 1, tp_count - 1, turn), tp_count)

    def forward(step, carry):
        at_z = near_first(z, step, tp_count)
        ahead = step + jnp.where(inside, 2, 1)

        @pl.when(ahead < tp_count)
        def _():
            next_z = near_first(z, ahead, tp_count)
            wait_row(side, next_z)
            spread(next_z)

        wait_row(other_y, at_z)
        pass_on(at_z).start()
        wait_row(other_core, at_z)
        wait_row(far_core, at_z)

        @pl.when(step == tp_count - 1)
        def _():
            back_y(return_order(0))

        count = side_count * own_rows
        block = piece(inner, 256)

        def hide(at, carry):
            columns = pl.ds(pl.multiple_of(at * block, block), block)
            taken = rows[:, at_z, :, :width].reshape(count, width)
            gate_sum = jnp.dot(taken, gate[:, columns], preferred_element_type=jnp.float32)
            upward = jnp.dot(taken, up[:, columns], preferred_element_type=jnp.float32)
            hidden[:, columns] = (gate_sum / (1.0 + jnp.exp(-gate_sum)) * upward).astype(
                jnp.bfloat16
            )
            return carry

        lax.fori_loop(0, inner // block, hide, 0)
        out_block = piece(width, 512)

        def show(at, carry):
            columns = pl.ds(pl.multiple_of(at * out_block, out_block), out_block)
            out = jnp.dot(hidden[...], down[:, columns], preferred_element_type=jnp.float32)
            listed = rows[:, at_z, :, width:].reshape(count, spare).astype(jnp.float32)
            lane = lax.broadcasted_iota(jnp.int32, (count, spare), 1)
            mine = jnp.logical_or(lane == me, lane == me + side_count * tp_count)
            scale = jnp.sum(jnp.where(mine, listed, 0.0), axis=1, keepdims=True)
            parts[:, at_z, :, columns] = (
                (out * scale).astype(jnp.bfloat16).reshape(side_count, own_rows, out_block)
            )
            return carry

        lax.fori_loop(0, width // out_block, show, 0)
        for at_y in range(side_count // 2):
            to_core(at_y, at_z).start()
        return carry

    lax.fori_loop(0, tp_count, forward, 0)

    def next_y(step, carry):
        back_y(return_order(step))
        return carry

    lax.fori_loop(1, tp_count, next_y, 0)

    def back_z(step, carry):
        at_z = return_order(step)
        to_y(at_z).wait_recv()
        add_to_part(side, at_z, from_y.at[at_z])
        to_line(at_z, z, at_z).start()
        return carry

    lax.fori_loop(0, tp_count - 1, back_z, 0)
    to_y(z).wait_recv()
    mix_ref[...] = parts[side, z].astype(jnp.float32) + from_y[z].astype(jnp.float32)

    def collect(step, carry):
        at_z = near_first(z, step, tp_count)
        to_line(at_z, at_z, at_z).wait_recv()
        mix_ref[...] += from_z[at_z].astype(jnp.float32)
        return carry

    lax.fori_loop(1, tp_count, collect, 0)

    def drain(at_z, carry):
        for condition, copy in line_sends(at_z):
            pl.when(condition)(copy.wait_send)
        for copy in side_sends(at_z):
            copy.wait_send()
        pass_on(at_z).wait_send()
        for at_y in range(side_count // 2):
            to_core(at_y, at_z).wait_send()
        to_y(at_z).wait_send()
        pl.when(at_z != z)(to_line(at_z, z, at_z).wait_send)
        return carry

    lax.fori_loop(0, tp_count, drain, 0)


def exchange_experts(normed, listed, gate_weight, up_weight, down_weight):
    side_count, tp_count = lax.axis_size("side"), lax.axis_size("tp")
    own_rows, width = normed.shape
    inner = gate_weight.shape[2]
    half = side_count // 2
    dma = pltpu.SemaphoreType.DMA
    block = (own_rows, width)
    flops = 6 * side_count * tp_count * own_rows * width * inner
    return pl.pallas_call(
        functools.partial(experts_kernel, side_count, tp_count),
        out_shape=jax.ShapeDtypeStruct(block, jnp.float32),
        in_specs=[pl.BlockSpec(memory_space=pltpu.VMEM)] * 2
        + [pl.BlockSpec(memory_space=pl.ANY)] * 3,
        out_specs=pl.BlockSpec(memory_space=pltpu.VMEM),
        scratch_shapes=[
            pltpu.VMEM((side_count, tp_count, own_rows, width + listed.shape[1]), jnp.bfloat16),
            pltpu.VMEM((side_count, tp_count) + block, jnp.bfloat16),
            pltpu.VMEM((half, tp_count) + block, jnp.bfloat16),
            pltpu.VMEM((tp_count,) + block, jnp.bfloat16),
            pltpu.VMEM((tp_count,) + block, jnp.bfloat16),
            pltpu.VMEM((width, inner), jnp.bfloat16),
            pltpu.VMEM((width, inner), jnp.bfloat16),
            pltpu.VMEM((inner, width), jnp.bfloat16),
            pltpu.VMEM((side_count * own_rows, inner), jnp.bfloat16),
            dma((3,)),
            dma((side_count, tp_count)),
            dma((tp_count,)),
            dma((tp_count,)),
            dma((tp_count,)),
            dma((2, tp_count)),
            dma((half, tp_count)),
            dma((half, tp_count)),
            dma((tp_count,)),
            dma((tp_count,)),
            dma((tp_count,)),
            dma((tp_count,)),
        ],
        compiler_params=pltpu.CompilerParams(
            collective_id=0, has_side_effects=True, vmem_limit_bytes=58 * 2**20
        ),
        cost_estimate=pl.CostEstimate(
            flops=flops, bytes_accessed=6 * width * inner, transcendentals=0
        ),
        name="experts_exchange",
    )(
        normed,
        listed,
        gate_weight,
        up_weight,
        down_weight,
    )


def dense_experts(
    stream, normed, gate_weight, up_weight, down_weight, expert_ids, numerators, experts_all
):
    weights = numerators.astype(jnp.float32)
    weights = weights / jnp.sum(weights, axis=1, keepdims=True)
    named = expert_ids[:, :, None] == jnp.arange(experts_all)[None, None, :]
    per_expert = jnp.sum(jnp.where(named, weights[:, :, None], 0.0), axis=1)
    if lax.axis_size("side") == 4 and 2 * experts_all <= 128:
        high = lax.reduce_precision(per_expert, 8, 7)
        spare = jnp.zeros((stream.shape[0], 128 - 2 * experts_all), jnp.float32)
        listed = jnp.concatenate([high, per_expert - high, spare], axis=1).astype(jnp.bfloat16)
        return stream + exchange_experts(normed, listed, gate_weight, up_weight, down_weight)
    all_weights = lax.all_gather(per_expert, ("side", "tp"), axis=0, tiled=True)
    me = lax.axis_index(("side", "tp"))
    own_weight = lax.dynamic_slice_in_dim(all_weights, me, 1, axis=1)
    rows = lax.all_gather(normed, ("side", "tp"), axis=0, tiled=True)
    gate_sum = jnp.dot(rows, gate_weight[0], preferred_element_type=jnp.float32)
    upward = jnp.dot(rows, up_weight[0], preferred_element_type=jnp.float32)
    hidden = (jax.nn.silu(gate_sum) * upward).astype(jnp.bfloat16)
    expert_out = jnp.dot(hidden, down_weight[0], preferred_element_type=jnp.float32)
    weighted = (expert_out * own_weight).astype(jnp.bfloat16)
    mixture = lax.psum_scatter(weighted, ("side", "tp"), scatter_dimension=0, tiled=True)
    return stream + mixture.astype(jnp.float32)


def attend_plain(
    queries, new_keys, new_values, cache_keys, cache_values, out_weight, residual, norm_gain
):
    group_rows = queries.shape[0]
    local_heads = queries.shape[1] // HD
    head_kv = (lax.axis_index("tp") * local_heads + jnp.arange(local_heads)) // (H // KV)
    query_heads = queries.reshape(group_rows, local_heads, HD)
    score_scale = 1.0 / math.sqrt(HD)
    initial = (
        jnp.full((local_heads, group_rows), -1e30, jnp.float32),
        jnp.zeros((local_heads, group_rows), jnp.float32),
        jnp.zeros((local_heads, group_rows, HD), jnp.float32),
    )
    cache_both = lax.all_gather(
        jnp.concatenate([cache_keys[0], cache_values[0]], axis=1), "tp", axis=0, tiled=True
    )
    key_width = cache_keys.shape[2]
    key_piece = pick_heads(cache_both[:, :key_width], head_kv)
    value_piece = pick_heads(cache_both[:, key_width:], head_kv)
    scores = (
        jnp.einsum("rhd,nhd->hrn", query_heads, key_piece, preferred_element_type=jnp.float32)
        * score_scale
    )
    state_now = softmax_update(initial, scores, value_piece)
    own_keys = pick_heads(new_keys, head_kv)
    own_values = pick_heads(new_values, head_kv)
    scores = (
        jnp.einsum("rhd,nhd->hrn", query_heads, own_keys, preferred_element_type=jnp.float32)
        * score_scale
    )
    positions = jnp.arange(group_rows)
    visible = positions[None, :] <= positions[:, None]
    scores = jnp.where(visible[None], scores, -1e30)
    running, totals, context = softmax_update(state_now, scores, own_values)
    attended = (
        (context / totals[..., None])
        .transpose(1, 0, 2)
        .reshape(group_rows, local_heads * HD)
        .astype(jnp.bfloat16)
    )
    own_rows = residual.shape[0]
    attn_out = lax.psum_scatter(
        jnp.dot(attended, out_weight, preferred_element_type=jnp.float32).astype(jnp.bfloat16),
        "tp",
        scatter_dimension=0,
        tiled=True,
    ).astype(jnp.float32)
    stream = residual.astype(jnp.float32) + attn_out
    normed = (
        stream
        * lax.rsqrt(jnp.mean(stream * stream, axis=-1, keepdims=True) + 1e-06)
        * norm_gain.astype(jnp.float32)
    ).astype(jnp.bfloat16)
    return stream, normed


def local(
    queries,
    new_keys,
    new_values,
    cache_keys,
    cache_values,
    out_weight,
    residual,
    norm_gain,
    gate_weight,
    up_weight,
    down_weight,
    expert_ids,
    numerators,
):
    tp_count = lax.axis_size("tp")
    side_count = lax.axis_size("side")
    own_rows = residual.shape[0]
    attend = attend_rows if tp_count == KV else attend_plain
    stream, normed = attend(
        queries, new_keys, new_values, cache_keys, cache_values, out_weight, residual, norm_gain
    )
    experts_all = side_count * tp_count
    top_count = expert_ids.shape[1]
    copies = own_rows * top_count
    capacity = max(2, 2 * copies // experts_all)
    if capacity >= own_rows:
        return dense_experts(
            stream, normed, gate_weight, up_weight, down_weight, expert_ids, numerators, experts_all
        )
    flat_ids = expert_ids.reshape(copies)
    one_hot = (flat_ids[:, None] == jnp.arange(experts_all)[None, :]).astype(jnp.int32)
    earlier = jnp.cumsum(one_hot, axis=0) - one_hot
    slot_rank = jnp.sum(earlier * one_hot, axis=1)
    slot_index = flat_ids * capacity + slot_rank
    owners = jnp.arange(copies) // top_count
    outgoing = (
        jnp.zeros((experts_all * capacity, D), jnp.bfloat16).at[slot_index].set(normed[owners])
    )
    outgoing = outgoing.reshape(experts_all, capacity, D)
    buffer = lax.all_to_all(outgoing, ("side", "tp"), split_axis=0, concat_axis=0, tiled=True)
    buffer_shape = buffer.shape
    flat_rows = buffer.reshape(-1, D)
    gate_sum = jnp.dot(flat_rows, gate_weight[0], preferred_element_type=jnp.float32)
    upward = jnp.dot(flat_rows, up_weight[0], preferred_element_type=jnp.float32)
    hidden = (jax.nn.silu(gate_sum) * upward).astype(jnp.bfloat16)
    returned = lax.all_to_all(
        jnp.dot(hidden, down_weight[0], preferred_element_type=jnp.float32)
        .astype(jnp.bfloat16)
        .reshape(buffer_shape),
        ("side", "tp"),
        split_axis=0,
        concat_axis=0,
        tiled=True,
    )
    gathered = returned.reshape(experts_all * capacity, D)[slot_index]
    weights = numerators.astype(jnp.float32)
    weights = weights / jnp.sum(weights, axis=1, keepdims=True)
    mixture = jnp.sum(
        weights[:, :, None] * gathered.reshape(own_rows, top_count, D).astype(jnp.float32), axis=1
    )
    return stream + mixture


def solution(mesh):
    in_specs = (
        P(("replica", "side"), "tp"),
        P(("replica", "side"), None),
        P(("replica", "side"), None),
        P(("replica", "side"), "tp", None),
        P(("replica", "side"), "tp", None),
        P("tp", None),
        P(("replica", "side", "tp"), None),
        P(),
        P(("side", "tp"), None, None),
        P(("side", "tp"), None, None),
        P(("side", "tp"), None, None),
        P(("replica", "side", "tp"), None),
        P(("replica", "side", "tp"), None),
    )
    out_specs = P(("replica", "side", "tp"), None)
    return jax.shard_map(local, mesh=mesh, in_specs=in_specs, out_specs=out_specs, check_vma=False)
```
